512 devices in a mesh: seq: 64 (over x, z), mp: 4 (over y), dp: 2 (over core).
Axes of the slice: x: 4, y: 4, z: 16, core: 2. Of those that a mesh axis runs over, the one named last changes fastest.
Arguments:
- queries: bfloat16 [2, 128, 64, 2048], P('dp', 'seq', None, 'mp'), may hold values from -6 to 6
- out_grad: bfloat16 [2, 128, 64, 2048], P('dp', 'seq', None, 'mp'), may hold values from -6 to 6
- encoded: bfloat16 [2, 256, 128, 896], P('dp', None, 'seq', 'mp'), may hold values from -6 to 6
- key_weight: bfloat16 [896, 2048], P(None, 'mp'), may hold values from -0.1875 to 0.1875
- value_weight: bfloat16 [896, 2048], P(None, 'mp'), may hold values from -0.1875 to 0.1875
- neighbour_ids: int32 [2, 128, 2], P('dp'), may hold values from 0 to 255
- neighbour_counts: int32 [2, 128], P('dp', 'seq'), may hold values from 1 to 2
Outputs:
- attended: bfloat16 [2, 128, 64, 2048], P('dp', 'seq', None, 'mp')
- query_grad: bfloat16 [2, 128, 64, 2048], P('dp', 'seq', None, 'mp')
- key_weight_grad: bfloat16 [896, 2048], P(None, ('mp', 'dp'))
- value_weight_grad: bfloat16 [896, 2048], P(None, ('mp', 'dp'))
The draws below stay inside these ranges and needn't reach their ends.
All inputs are finite; a program needn't handle non-finite values.
Results may differ from the reference program's by a relative error of at most 0.017.
Values may be sent and summed in bfloat16 or wider, within the bound.
A program may use at most 64 MiB of HBM per device.

```python
import jax
import jax.numpy as jnp

HEADS = 16
HD = 128
E = 896
CH = 64
NL = 128
NBR = 2
HF = 2048
STRETCHES = 128
NEIGH = 256
N_DP = 2


def touch_ends(values, own_key, low, high):
    place = [jax.random.randint(jax.random.fold_in(own_key, axis), (), 0, length) for axis, length in enumerate(values.shape)]
    widest = values.shape.index(max(values.shape))
    beside = place[:widest] + [(place[widest] + 1) % values.shape[widest]] + place[widest + 1:]
    return values.at[tuple(place)].set(low).at[tuple(beside)].set(high)


def shard_levels(key, dims, split, least, largest):
    def one(dim, parts):
        heights = jax.random.uniform(jax.random.fold_in(jax.random.fold_in(key, 6), dim), (parts,), jnp.float32, least / len(split), largest / len(split))
        return jnp.repeat(jnp.exp(heights), dims[dim] // parts).reshape((-1,) + (1,) * (len(dims) - dim - 1))

    level = one(*split[0])
    for cut in split[1:]:
        level = level * one(*cut)
    return level


def bell_draw(stream_key, extent, deviation, most, split=(), kind=jnp.bfloat16):
    loudness = shard_levels(stream_key, extent, split, -0.22, 0.18) if split else 1.0
    result = jax.random.normal(stream_key, extent, jnp.float32) * deviation * loudness
    return jnp.minimum(jnp.maximum(result, -most), most).astype(kind)


def setup_inputs(seed: int = 0) -> dict:
    splits = jax.random.split(jax.random.key(seed), 8)
    return {
        "queries": bell_draw(splits[0], (N_DP, STRETCHES, CH, HF), 1.0, 6.0, ((0, 2), (1, 64), (3, 4))),
        "out_grad": bell_draw(splits[1], (N_DP, STRETCHES, CH, HF), 1.0, 6.0, ((0, 2), (1, 64), (3, 4))),
        "encoded": bell_draw(splits[2], (N_DP, NEIGH, NL, E), 1.0, 6.0, ((0, 2), (2, 64), (3, 4))),
        "key_weight": bell_draw(splits[3], (E, HF), E ** -0.5, 0.1875, ((1, 4),)),
        "value_weight": bell_draw(splits[4], (E, HF), E ** -0.5, 0.1875, ((1, 4),)),
        "neighbour_ids": touch_ends(jax.random.randint(splits[5], (N_DP, STRETCHES, NBR), 0, NEIGH), jax.random.fold_in(splits[5], 1), 0, NEIGH - 1).astype(jnp.int32),
        "neighbour_counts": touch_ends(jax.random.randint(splits[6], (N_DP, STRETCHES), 1, NBR + 1), jax.random.fold_in(splits[6], 1), 1, NBR).astype(jnp.int32),
    }


def reference(queries, out_grad, encoded, key_weight, value_weight, neighbour_ids, neighbour_counts):
    weights = jnp.concatenate([key_weight, value_weight], axis=1)
    scale = HD ** -0.5
    grad_total = jnp.zeros((E, 2 * HF), jnp.float32)
    attended_all = []
    query_all = []
    for group in range(N_DP):
        rows = encoded[group][neighbour_ids[group].reshape(-1)]
        flat_rows = rows.reshape(-1, E)
        kv = jnp.dot(flat_rows, weights, preferred_element_type=jnp.float32).astype(jnp.bfloat16)
        kv = kv.reshape(STRETCHES, NBR * NL, 2 * HF)
        keys = kv[:, :, :HF].reshape(STRETCHES, NBR * NL, HEADS, HD).astype(jnp.float32)
        values = kv[:, :, HF:].reshape(STRETCHES, NBR * NL, HEADS, HD).astype(jnp.float32)
        query = queries[group].reshape(STRETCHES, CH, HEADS, HD).astype(jnp.float32)
        grad_out = out_grad[group].reshape(STRETCHES, CH, HEADS, HD).astype(jnp.float32)
        slot = jnp.arange(NBR * NL, dtype=jnp.int32) // NL
        valid = slot[None, :] < neighbour_counts[group][:, None]
        scores = jnp.einsum("cqhd,ckhd->chqk", query, keys) * scale
        scores = jnp.where(valid[:, None, None, :], scores, -1e30)
        top = jnp.max(scores, axis=-1, keepdims=True)
        expo = jnp.exp(scores - top)
        probs = expo / jnp.sum(expo, axis=-1, keepdims=True)
        probs_low = probs.astype(jnp.bfloat16).astype(jnp.float32)
        heads_out = jnp.einsum("chqk,ckhd->cqhd", probs_low, values)
        attended_all.append(heads_out.astype(jnp.bfloat16).reshape(STRETCHES, CH, HF))
        grad_probs = jnp.einsum("cqhd,ckhd->chqk", grad_out, values)
        delta = jnp.einsum("cqhd,cqhd->chq", grad_out, heads_out)
        grad_scores = probs * (grad_probs - delta[..., None])
        grad_low = grad_scores.astype(jnp.bfloat16).astype(jnp.float32)
        query_grad = jnp.einsum("chqk,ckhd->cqhd", grad_low, keys) * scale
        query_all.append(query_grad.astype(jnp.bfloat16).reshape(STRETCHES, CH, HF))
        key_grad = (jnp.einsum("chqk,cqhd->ckhd", grad_low, query) * scale).astype(jnp.bfloat16)
        value_grad = jnp.einsum("chqk,cqhd->ckhd", probs_low, grad_out).astype(jnp.bfloat16)
        slot_grad = jnp.concatenate([key_grad.reshape(-1, HF), value_grad.reshape(-1, HF)], axis=1)
        grad_total = grad_total + jnp.dot(flat_rows.T, slot_grad, preferred_element_type=jnp.float32)
    grad_low_out = grad_total.astype(jnp.bfloat16)
    return (jnp.stack(attended_all), jnp.stack(query_all), grad_low_out[:, :HF], grad_low_out[:, HF:])
```

```python
import functools

import jax
import jax.numpy as jnp
from jax import lax
from jax.experimental import pallas as pl
from jax.experimental.pallas import tpu as pltpu
from jax.sharding import PartitionSpec as P

HD = 128
NX, NZ, NM = 4, 16, 4
MESH = pl.DeviceIdType.MESH
BF = jnp.bfloat16
F32 = jnp.float32
SHIFT = [0] + [(p + 1) // 2 if p % 2 else NZ - p // 2 for p in range(1, NZ)]


def dot(a, b, dims):
    return lax.dot_general(a, b, ((dims[:1], dims[1:]), ((), ())), preferred_element_type=F32)


def wait_bytes(ref, sem):
    pltpu.make_async_copy(ref, ref, sem).wait()


def kernel(
    idx_ref, counts_ref, enc_ref, q_hbm, og_hbm, wk_hbm, wv_hbm,
    att_ref, qg_ref, wg_ref,
    w, q, og, outgoing, zbuf, rows, rows_t, kv, sg, dps, dpr, hf, xs, xr, zf, zs, zr,
    load_sem, send_sem, az_sem, ax_sem, ay_sem, dp_sem, rx_sem, rz_sem, gz_sem, gx_sem,
):
    seq = lax.axis_index("seq")
    m = lax.axis_index("mp")
    d = lax.axis_index("dp")
    x, z = seq // NZ, lax.rem(seq, NZ)
    ze, zj = lax.rem(z, 4), z // 4

    def along_z(k):
        return {"seq": x * NZ + lax.rem(z + k, NZ)}

    def along_x(k):
        return {"seq": lax.rem(x + k, NX) * NZ + z}

    def along_m(k):
        return {"mp": lax.rem(m + k, NM)}

    sibling = {"dp": 1 - d}

    def send(src, dst, phase, recv, device):
        pltpu.make_async_remote_copy(
            src_ref=src, dst_ref=dst, send_sem=send_sem.at[phase], recv_sem=recv,
            device_id=device, device_id_type=MESH,
        ).start()

    barrier = pltpu.get_barrier_semaphore()
    peers = [along_z(k) for k in range(1, NZ)] + [along_x(k) for k in range(1, NX)]
    peers += [along_m(k) for k in range(1, NM)] + [sibling]
    for peer in peers:
        pl.semaphore_signal(barrier, inc=1, device_id=peer, device_id_type=MESH)

    loads = []
    for e in range(NM):
        for half, hbm in enumerate((wk_hbm, wv_hbm)):
            loads.append(pltpu.make_async_copy(
                hbm.at[pl.ds(224 * e, 224)],
                w.at[pl.ds(256 * e, 224), pl.ds(512 * half, 512)],
                load_sem.at[len(loads)],
            ))
    loads.append(pltpu.make_async_copy(q_hbm, q, load_sem.at[8]))
    loads.append(pltpu.make_async_copy(og_hbm, og, load_sem.at[9]))
    for load in loads:
        load.start()
    for e in range(NM):
        w[pl.ds(256 * e + 224, 32), :] = jnp.zeros((32, 1024), BF)

    place = lax.broadcasted_iota(jnp.int32, (512, 512), 0)
    chosen = jnp.where(place == idx_ref[...], 1.0, 0.0).astype(BF)
    outgoing[...] = dot(chosen, enc_ref[...], (0, 0)).astype(BF).reshape(NZ, NX, 8, 256)
    zbuf[0] = outgoing[z]

    pl.semaphore_wait(barrier, len(peers))

    for p in range(1, NZ):
        send(outgoing.at[lax.rem(z + SHIFT[p], NZ)], zbuf.at[p], 0, az_sem.at[p // 4], along_z(SHIFT[p]))
    mine = pl.ds(pl.multiple_of(m * 256, 256), 256)

    def to_x(g):
        low = max(4 * g, 1)
        wait_bytes(zbuf.at[pl.ds(low, 4 * g + 4 - low)], az_sem.at[g])
        for s in range(1, NX):
            send(zbuf.at[pl.ds(4 * g, 4), lax.rem(x + s, NX)], rows.at[g, s, :, :, mine], 1, ax_sem.at[g], along_x(s))
        rows[g, 0, :, :, mine] = zbuf[pl.ds(4 * g, 4), x]

    def to_m(g):
        wait_bytes(rows.at[g, pl.ds(1, 3), :, :, mine], ax_sem.at[g])
        for t in range(1, NM):
            send(rows.at[g, :, :, :, mine], rows.at[g, :, :, :, mine], 2, ay_sem.at[g], along_m(t))

    to_x(0)
    for g in range(1, 4):
        to_x(g)
        to_m(g - 1)
    to_m(3)
    for load in loads:
        load.wait()
    for g in range(4):
        wait_bytes(rows.at[g, :, :, :, pl.ds(0, 768)], ay_sem.at[g])

    flat = rows[...].reshape(512, 1024)
    for c in range(4):
        cols = pl.ds(256 * c, 256)
        kv[:, cols] = dot(flat, w[:, cols], (1, 0)).astype(BF)
    rows_t[...] = flat.T

    scale = HD ** (-0.5)
    key = lax.broadcasted_iota(jnp.int32, (128, 512), 1)
    owner = lax.broadcasted_iota(jnp.int32, (128, 512), 0) // 64
    count = jnp.where(owner == 0, counts_ref[0, 0], counts_ref[0, 1])
    valid = (((key // 2) & 1) == owner) & ((key & 1) < count)
    for h in range(4):
        cols = pl.ds(HD * h, HD)
        vcols = pl.ds(512 + HD * h, HD)
        qh, gh, kh, vh = q[:, cols], og[:, cols], kv[:, cols], kv[:, vcols]
        scores = jnp.where(valid, dot(qh, kh, (1, 1)) * scale, -1e30)
        expo = jnp.exp(scores - jnp.max(scores, axis=-1, keepdims=True))
        probs = expo * (1.0 / jnp.sum(expo, axis=-1, keepdims=True))
        low = probs.astype(BF)
        heads = dot(low, vh, (1, 0))
        att_ref[:, cols] = heads.astype(BF)
        delta = jnp.sum(gh.astype(F32) * heads, axis=-1, keepdims=True)
        grad = (probs * (dot(gh, vh, (1, 1)) - delta)).astype(BF)
        qg_ref[:, cols] = (dot(grad, kh, (1, 0)) * scale).astype(BF)
        sg[:, cols] = (dot(grad, qh, (0, 0)) * scale).astype(BF)
        sg[:, vcols] = dot(low, gh, (0, 0)).astype(BF)

    def partial(e, side, half):
        cols = pl.ds(pl.multiple_of(512 * half + 256 * side, 256), 256)
        return dot(rows_t[pl.ds(256 * e, 256), :], sg[:, cols], (1, 0))[:224]

    for e in range(4):
        for half in range(2):
            part = partial(e, 1 - d, half)
            for c in range(2):
                dps[e, 2 * half + c] = part[:, 128 * c:128 * c + 128].reshape(4, 56, 128).astype(BF)
        send(dps.at[e], dpr.at[e], 3, dp_sem.at[e], sibling)
    for e in range(4):
        parts = [partial(e, d, half) for half in range(2)]
        wait_bytes(dpr.at[e], dp_sem.at[e])
        for half in range(2):
            for c in range(2):
                tile = 2 * half + c
                both = parts[half][:, 128 * c:128 * c + 128].reshape(4, 56, 128) + dpr[e, tile].astype(F32)
                hf[tile, e] = both
                xs[tile, e] = both.astype(BF)
        for s in range(1, NX):
            send(xs.at[lax.rem(x + s, NX), e], xr.at[s - 1, e], 4, rx_sem.at[e], along_x(s))
    for e in range(4):
        wait_bytes(xr.at[:, e], rx_sem.at[e])
        total = hf[x, e] + xr[0, e].astype(F32) + xr[1, e].astype(F32) + xr[2, e].astype(F32)
        zf[e] = total
        zs[e] = total.astype(BF)
        for i in range(4):
            j = lax.rem(zj + i, 4)
            ahead = lax.rem(4 * j + e - z + NZ, NZ)

            def go():
                send(zs.at[e, j], zr.at[15 - ahead], 5, rz_sem.at[0], along_z(ahead))

            if i == 0:
                pl.when(ze != e)(go)
            else:
                go()
    wait_bytes(zr, rz_sem.at[0])
    total = zf[ze, zj]
    for k in range(NZ - 1):
        total += zr[k].astype(F32)
    own = 4 * ze + zj
    wg_ref[x, own] = total.astype(BF)
    for k in range(1, NZ):
        send(wg_ref.at[x, own], wg_ref.at[x, own], 6, gz_sem.at[ze], along_z(SHIFT[k]))
    for e in range(4):
        @pl.when(ze == e)
        def _():
            wait_bytes(zr.at[pl.ds(0, 3)], gz_sem.at[e])

        @pl.when(ze != e)
        def _():
            wait_bytes(zr.at[pl.ds(0, 4)], gz_sem.at[e])

        for s in range(1, NX):
            block = wg_ref.at[x, pl.ds(4 * e, 4)]
            send(block, block, 7, gx_sem.at[0], along_x(s))
    wait_bytes(xr, gx_sem.at[0])

    wait_bytes(zbuf.at[pl.ds(1, 15)], send_sem.at[0])
    wait_bytes(zbuf.at[pl.ds(0, 12)], send_sem.at[1])
    wait_bytes(rows.at[:, :, :, :, pl.ds(0, 768)], send_sem.at[2])
    wait_bytes(dps, send_sem.at[3])
    wait_bytes(xr, send_sem.at[4])
    wait_bytes(zr, send_sem.at[5])
    wait_bytes(zr, send_sem.at[6])
    wait_bytes(xr, send_sem.at[7])


def body(queries, out_grad, encoded, key_weight, value_weight, neighbour_ids, neighbour_counts):
    enc = jnp.pad(encoded[0].reshape(512, 224), ((0, 0), (0, 32)))
    ids = neighbour_ids[0].reshape(NX, NZ, 1, 4).transpose(1, 0, 2, 3)
    token = jnp.arange(2, dtype=jnp.int32).reshape(1, 1, 2, 1)
    idx = (2 * ids + token).reshape(1, 512)
    vmem = pl.BlockSpec(memory_space=pltpu.VMEM)
    hbm = pl.BlockSpec(memory_space=pl.ANY)
    dma = pltpu.SemaphoreType.DMA
    att, qg, wg = pl.pallas_call(
        kernel,
        out_shape=(
            jax.ShapeDtypeStruct((128, 512), BF),
            jax.ShapeDtypeStruct((128, 512), BF),
            jax.ShapeDtypeStruct((4, 16, 56, 128), BF),
        ),
        in_specs=[vmem, pl.BlockSpec(memory_space=pltpu.SMEM), vmem, hbm, hbm, hbm, hbm],
        out_specs=(vmem, vmem, vmem),
        scratch_shapes=[
            pltpu.VMEM((1024, 1024), BF),
            pltpu.VMEM((128, 512), BF),
            pltpu.VMEM((128, 512), BF),
            pltpu.VMEM((NZ, NX, 8, 256), BF),
            pltpu.VMEM((NZ, NX, 8, 256), BF),
            pltpu.VMEM((4, NX, 4, 8, 1024), BF),
            pltpu.VMEM((1024, 512), BF),
            pltpu.VMEM((512, 1024), BF),
            pltpu.VMEM((512, 1024), BF),
            pltpu.VMEM((4, 4, 4, 56, 128), BF),
            pltpu.VMEM((4, 4, 4, 56, 128), BF),
            pltpu.VMEM((4, 4, 4, 56, 128), F32),
            pltpu.VMEM((4, 4, 4, 56, 128), BF),
            pltpu.VMEM((3, 4, 4, 56, 128), BF),
            pltpu.VMEM((4, 4, 56, 128), F32),
            pltpu.VMEM((4, 4, 56, 128), BF),
            pltpu.VMEM((15, 56, 128), BF),
            dma((10,)), dma((8,)), dma((4,)), dma((4,)), dma((4,)),
            dma((4,)), dma((4,)), dma((1,)), dma((4,)), dma((1,)),
        ],
        compiler_params=pltpu.CompilerParams(
            collective_id=0, has_side_effects=True, vmem_limit_bytes=56 * 1024 * 1024
        ),
        cost_estimate=pl.CostEstimate(flops=2_500_000_000, bytes_accessed=4_000_000, transcendentals=262144),
    )(
        idx, neighbour_counts, enc,
        queries.reshape(128, 512), out_grad.reshape(128, 512), key_weight, value_weight,
    )
    grads = wg.reshape(4, 896, 128)
    kwg = jnp.concatenate([grads[0], grads[1]], axis=1)
    vwg = jnp.concatenate([grads[2], grads[3]], axis=1)
    return att.reshape(1, 2, 64, 512), qg.reshape(1, 2, 64, 512), kwg, vwg


def solution(mesh):
    return jax.shard_map(
        body,
        mesh=mesh,
        in_specs=(
            P("dp", "seq", None, "mp"),
            P("dp", "seq", None, "mp"),
            P("dp", None, "seq", "mp"),
            P(None, "mp"),
            P(None, "mp"),
            P("dp", None, None),
            P("dp", "seq"),
        ),
        out_specs=(
            P("dp", "seq", None, "mp"),
            P("dp", "seq", None, "mp"),
            P(None, ("mp", "dp")),
            P(None, ("mp", "dp")),
        ),
        check_vma=False,
    )
```

```python
import functools

import jax
import jax.numpy as jnp
from jax import lax
from jax.experimental import pallas as pl
from jax.experimental.pallas import tpu as pltpu
from jax.sharding import PartitionSpec as P

HD = 128
NX, NZ, NM = 4, 16, 4
MESH = pl.DeviceIdType.MESH
BF = jnp.bfloat16
F32 = jnp.float32
SHIFT = [0] + [(p + 1) // 2 if p % 2 else NZ - p // 2 for p in range(1, NZ)]


def dot(a, b, dims):
    return lax.dot_general(a, b, ((dims[:1], dims[1:]), ((), ())), preferred_element_type=F32)


def wait_bytes(ref, sem):
    pltpu.make_async_copy(ref, ref, sem).wait()


GROUPS = ((0, 6), (6, 11), (11, 14), (14, 16))
RA, RB = 32, 24


def kernel(
    ids_ref, counts_ref, enc_ref, q_hbm, og_hbm, wk_hbm, wv_hbm,
    att_hbm, qg_hbm, ga, gb,
    w, q, og, att, qg, outgoing, zbuf, rows, rows_t, kv, sg, dps, dpr,
    ha, hb, xsa, zsb, xra, znb, zfa, zsa, zna, hbx, xsb, xrb, ffa, fsa, fra, ffb, fsb, frb,
    load_sem, send_sem, az_sem, ax_sem, ay_sem, dp_sem, rxa_sem, one_sem, gna_sem,
):
    seq = lax.axis_index("seq")
    m = lax.axis_index("mp")
    d = lax.axis_index("dp")
    x, z = seq // NZ, lax.rem(seq, NZ)
    ze, zj = lax.rem(z, 4), z // 4

    def along_z(k):
        return {"seq": x * NZ + lax.rem(z + (k + NZ) % NZ, NZ)}

    def along_x(k):
        return {"seq": lax.rem(x + k, NX) * NZ + z}

    def along_m(k):
        return {"mp": lax.rem(m + k, NM)}

    sibling = {"dp": 1 - d}

    def send(src, dst, phase, recv, device):
        pltpu.make_async_remote_copy(
            src_ref=src, dst_ref=dst, send_sem=send_sem.at[phase], recv_sem=recv,
            device_id=device, device_id_type=MESH,
        ).start()

    barrier = pltpu.get_barrier_semaphore()
    peers = [along_z(k) for k in range(1, NZ)] + [along_x(k) for k in range(1, NX)]
    peers += [along_m(k) for k in range(1, NM)] + [sibling]
    for peer in peers:
        pl.semaphore_signal(barrier, inc=1, device_id=peer, device_id_type=MESH)

    loads = []
    for e in range(NM):
        for half, hbm in enumerate((wk_hbm, wv_hbm)):
            loads.append(pltpu.make_async_copy(
                hbm.at[pl.ds(224 * e, 224)],
                w.at[pl.ds(256 * e, 224), pl.ds(512 * half, 512)],
                load_sem.at[len(loads)],
            ))
    loads.append(pltpu.make_async_copy(q_hbm, q, load_sem.at[8]))
    loads.append(pltpu.make_async_copy(og_hbm, og, load_sem.at[9]))
    for load in loads:
        load.start()

    lane = lax.broadcasted_iota(jnp.int32, (128, 512), 1)
    part = lax.broadcasted_iota(jnp.int32, (128, 512), 0)
    stretch = ((lane // 8) % NX) * (2 * NZ) + (lane // 32) * 2 + (lane // 2) % 2
    wanted = jnp.zeros((8, 512), F32)
    for slot in range(2):
        pick = jnp.where((part == stretch) & (lane % 2 == slot), 1.0, 0.0).astype(BF)
        ids = jnp.broadcast_to(ids_ref[pl.ds(slot, 1), :], (8, 128)).astype(F32).astype(BF)
        wanted += dot(ids, pick, (1, 0))
    wanted = wanted[:1].astype(jnp.int32)
    place = lax.broadcasted_iota(jnp.int32, (256, 512), 0)
    token = (lax.broadcasted_iota(jnp.int32, (1, 512), 1) // 4) % 2
    found = jnp.zeros((224, 512), F32)
    for t in range(2):
        chosen = jnp.where(place == jnp.where(token == t, wanted, -1), 1.0, 0.0).astype(BF)
        found += dot(enc_ref[t], chosen, (1, 0))
    found = jnp.concatenate([found, jnp.zeros((32, 512), F32)], axis=0)
    outgoing[...] = found.T.astype(BF).reshape(NZ, NX, 8, 256)
    zbuf[0] = outgoing[z]

    pl.semaphore_wait(barrier, len(peers))

    group_of = [g for g, (low, high) in enumerate(GROUPS) for _ in range(low, high)]
    for p in range(1, NZ):
        send(outgoing.at[lax.rem(z + SHIFT[p], NZ)], zbuf.at[p], 0, az_sem.at[group_of[p]], along_z(SHIFT[p]))
    for e in range(NM):
        w[pl.ds(256 * e + 224, 32), :] = jnp.zeros((32, 1024), BF)
    mine = pl.ds(pl.multiple_of(m * 256, 256), 256)

    def to_x(g):
        low, high = GROUPS[g]
        some = pl.ds(low, high - low)
        first = max(low, 1)
        wait_bytes(zbuf.at[pl.ds(first, high - first)], az_sem.at[g])
        for s in range(1, NX):
            send(zbuf.at[some, lax.rem(x + s, NX)], rows.at[some, s, :, mine], 1, ax_sem.at[g], along_x(s))
        rows[some, 0, :, mine] = zbuf[some, x]

    def to_m(g):
        low, high = GROUPS[g]
        some = pl.ds(low, high - low)
        wait_bytes(rows.at[some, pl.ds(1, 3), :, mine], ax_sem.at[g])
        for t in range(1, NM):
            send(rows.at[some, :, :, mine], rows.at[some, :, :, mine], 2, ay_sem.at[g], along_m(t))

    to_x(0)
    for g in range(1, len(GROUPS)):
        to_x(g)
        to_m(g - 1)
    to_m(len(GROUPS) - 1)
    for load in loads:
        load.wait()
    for g, (low, high) in enumerate(GROUPS):
        wait_bytes(rows.at[pl.ds(low, high - low), :, :, pl.ds(0, 768)], ay_sem.at[g])

    flat = rows[...].reshape(512, 1024)
    for c in range(4):
        cols = pl.ds(256 * c, 256)
        kv[:, cols] = dot(flat, w[:, cols], (1, 0)).astype(BF)
    rows_t[...] = flat.T

    scale = HD ** (-0.5)
    key = lax.broadcasted_iota(jnp.int32, (128, 512), 1)
    owner = lax.broadcasted_iota(jnp.int32, (128, 512), 0) // 64
    count = jnp.where(owner == 0, counts_ref[0, 0], counts_ref[0, 1])
    valid = (((key // 2) & 1) == owner) & ((key & 1) < count)
    for h in range(4):
        cols = pl.ds(HD * h, HD)
        vcols = pl.ds(512 + HD * h, HD)
        qh, gh, kh, vh = q[:, cols], og[:, cols], kv[:, cols], kv[:, vcols]
        scores = jnp.where(valid, dot(qh, kh, (1, 1)) * scale, -1e30)
        expo = jnp.exp(scores - jnp.max(scores, axis=-1, keepdims=True))
        probs = expo * (1.0 / jnp.sum(expo, axis=-1, keepdims=True))
        low = probs.astype(BF)
        heads = dot(low, vh, (1, 0))
        att[:, cols] = heads.astype(BF)
        delta = jnp.sum(gh.astype(F32) * heads, axis=-1, keepdims=True)
        grad = (probs * (dot(gh, vh, (1, 1)) - delta)).astype(BF)
        qg[:, cols] = (dot(grad, kh, (1, 0)) * scale).astype(BF)
        sg[:, cols] = (dot(grad, qh, (0, 0)) * scale).astype(BF)
        sg[:, vcols] = dot(low, gh, (0, 0)).astype(BF)
    stores = [
        pltpu.make_async_copy(att, att_hbm, load_sem.at[0]),
        pltpu.make_async_copy(qg, qg_hbm, load_sem.at[1]),
    ]
    for store in stores:
        store.start()

    def partial(e, side, half):
        cols = pl.ds(pl.multiple_of(512 * half + 256 * side, 256), 256)
        return dot(rows_t[pl.ds(256 * e, 256), :], sg[:, cols], (1, 0))[:224]

    def to_class(k, whole, first, second, src, dst, phase, sem):
        @pl.when(k == 1)
        def _():
            send(src(whole), dst(0, whole), phase, sem, along_z(1))

        @pl.when(k == 3)
        def _():
            send(src(whole), dst(1, whole), phase, sem, along_z(-1))

        @pl.when(k == 2)
        def _():
            send(src(first), dst(2, first), phase, sem, along_z(2))
            send(src(second), dst(2, second), phase, sem, along_z(-2))

    whole, first, second = pl.ds(0, 4), pl.ds(0, 2), pl.ds(2, 2)
    for e in range(4):
        for half in range(2):
            part = partial(e, 1 - d, half)
            for c in range(2):
                dps[e, 2 * half + c] = part[:, 128 * c:128 * c + 128].reshape(4, 56, 128).astype(BF)
        send(dps.at[e], dpr.at[e], 3, dp_sem.at[e], sibling)
    for e in range(4):
        parts = [partial(e, d, half) for half in range(2)]
        wait_bytes(dpr.at[e], dp_sem.at[e])
        for half in range(2):
            for c in range(2):
                tile = 2 * half + c
                both = parts[half][:, 128 * c:128 * c + 128].reshape(4, 56, 128) + dpr[e, tile].astype(F32)
                ha[tile, e], hb[e, tile] = both[:, :RA], both[:, RA:]
                xsa[tile, e], zsb[e, tile] = both[:, :RA].astype(BF), both[:, RA:].astype(BF)
        for s in range(1, NX):
            send(xsa.at[lax.rem(x + s, NX), e], xra.at[s - 1, e], 4, rxa_sem.at[e], along_x(s))
        to_class(
            lax.rem(e - ze + 4, 4), whole, first, second,
            lambda some: zsb.at[e, some], lambda slot, some: znb.at[slot, some], 5, one_sem.at[0],
        )

    def add(base, received, *where):
        for s in range(3):
            base += received[(s, *where)].astype(F32)
        return base

    def fold_a(e):
        wait_bytes(xra.at[:, e], rxa_sem.at[e])
        total = add(ha[x, e], xra, e)
        zfa[e] = total
        zsa[e] = total.astype(BF)
        to_class(
            lax.rem(e - ze + 4, 4), whole, first, second,
            lambda some: zsa.at[e, some], lambda slot, some: zna.at[slot, some], 6, one_sem.at[1],
        )

    fold_a(0)
    fold_a(1)
    wait_bytes(znb, one_sem.at[0])
    for tile in range(4):
        total = add(hb[ze, tile], znb, tile)
        hbx[tile] = total
        xsb[tile] = total.astype(BF)
    for s in range(1, NX):
        send(xsb.at[lax.rem(x + s, NX)], xrb.at[s - 1], 7, one_sem.at[2], along_x(s))
    fold_a(2)
    fold_a(3)
    wait_bytes(xrb, one_sem.at[2])
    total = add(hbx[x], xrb)
    ffb[...] = total
    fsb[...] = total.astype(BF)
    for i in range(1, 4):
        send(fsb.at[lax.rem(zj + i, 4)], frb.at[i - 1], 9, one_sem.at[4], along_z(4 * i))
    wait_bytes(zna, one_sem.at[1])
    total = add(zfa[ze], zna)
    ffa[...] = total
    fsa[...] = total.astype(BF)
    for i in range(1, 4):
        send(fsa.at[lax.rem(zj + i, 4)], fra.at[i - 1], 8, one_sem.at[3], along_z(4 * i))
    wait_bytes(frb, one_sem.at[4])
    gb[ze, x, zj] = add(ffb[zj], frb).astype(BF)
    for i in range(1, 4):
        send(gb.at[ze, x, zj], gb.at[ze, x, zj], 11, one_sem.at[6], along_z(4 * i))
    wait_bytes(fra, one_sem.at[3])
    ga[x, ze, zj] = add(ffa[zj], fra).astype(BF)
    for i in range(1, 4):
        send(ga.at[x, ze, zj], ga.at[x, ze, zj], 10, one_sem.at[5], along_z(4 * i))

    wait_bytes(frb, one_sem.at[6])
    for s in range(1, NX):
        send(gb.at[ze, x], gb.at[ze, x], 14, one_sem.at[8], along_x(s))
    wait_bytes(fra, one_sem.at[5])
    for i, (shift, some) in enumerate(((1, whole), (-1, whole), (2, first), (-2, second))):
        send(ga.at[x, ze, some], ga.at[x, ze, some], 12, gna_sem.at[min(i, 2)], along_z(shift))
    for s in range(1, NX):
        send(ga.at[x, ze], ga.at[x, ze], 13, one_sem.at[7], along_x(s))
    wait_bytes(xrb, one_sem.at[8])
    for shift, some in ((1, whole), (-1, whole), (2, first), (-2, second)):
        send(gb.at[ze, some], gb.at[ze, some], 15, one_sem.at[9], along_z(shift))
    for i, k in enumerate((3, 1, 2)):
        wait_bytes(zna.at[i], gna_sem.at[i])
        group = lax.rem(ze + k, 4)
        for s in range(1, NX):
            send(ga.at[x, group], ga.at[x, group], 13, one_sem.at[7], along_x(s))
    wait_bytes(znb, one_sem.at[9])
    wait_bytes(xra, one_sem.at[7])

    for store in stores:
        store.wait()
    wait_bytes(zbuf.at[pl.ds(1, 15)], send_sem.at[0])
    wait_bytes(rows.at[:, pl.ds(1, 3), :, pl.ds(0, 256)], send_sem.at[1])
    wait_bytes(rows.at[:, :, :, pl.ds(0, 768)], send_sem.at[2])
    for phase, sized in enumerate((dps, xra, znb, zna, xrb, fra, frb, fra, frb, zna, xra, xrb, znb)):
        wait_bytes(sized, send_sem.at[phase + 3])


def place(att_in, qg_in, ga, gb, att_out, qg_out, kg_out, vg_out):
    att_out[...] = att_in[...]
    qg_out[...] = qg_in[...]
    for tile in range(4):
        out = (kg_out, vg_out)[tile // 2]
        lanes = pl.ds(128 * (tile % 2), 128)
        out[:, :, pl.ds(0, RA), lanes] = ga[tile]
        out[:, :, pl.ds(RA, RB), lanes] = gb[:, tile]


def body(queries, out_grad, encoded, key_weight, value_weight, neighbour_ids, neighbour_counts):
    vmem = pl.BlockSpec(memory_space=pltpu.VMEM)
    hbm = pl.BlockSpec(memory_space=pl.ANY)
    dma = pltpu.SemaphoreType.DMA

    def bf(*shape):
        return pltpu.VMEM(shape, BF)

    def f32(*shape):
        return pltpu.VMEM(shape, F32)

    low = jax.ShapeDtypeStruct((128, 512), BF)
    att, qg, ga, gb = pl.pallas_call(
        kernel,
        out_shape=(
            low, low,
            jax.ShapeDtypeStruct((4, 4, 4, RA, 128), BF),
            jax.ShapeDtypeStruct((4, 4, 4, RB, 128), BF),
        ),
        in_specs=[vmem, pl.BlockSpec(memory_space=pltpu.SMEM), vmem, hbm, hbm, hbm, hbm],
        out_specs=(hbm, hbm, vmem, vmem),
        scratch_shapes=[
            bf(1024, 1024), bf(128, 512), bf(128, 512), bf(128, 512), bf(128, 512),
            bf(NZ, NX, 8, 256), bf(NZ, NX, 8, 256),
            bf(NZ, NX, 8, 1024), bf(1024, 512), bf(512, 1024), bf(512, 1024),
            bf(4, 4, 4, 56, 128), bf(4, 4, 4, 56, 128),
            f32(4, 4, 4, RA, 128), f32(4, 4, 4, RB, 128),
            bf(4, 4, 4, RA, 128), bf(4, 4, 4, RB, 128),
            bf(3, 4, 4, RA, 128), bf(3, 4, 4, RB, 128),
            f32(4, 4, RA, 128), bf(4, 4, RA, 128), bf(3, 4, RA, 128),
            f32(4, 4, RB, 128), bf(4, 4, RB, 128), bf(3, 4, RB, 128),
            f32(4, RA, 128), bf(4, RA, 128), bf(3, RA, 128),
            f32(4, RB, 128), bf(4, RB, 128), bf(3, RB, 128),
            dma((10,)), dma((16,)), dma((4,)), dma((4,)), dma((4,)),
            dma((4,)), dma((4,)), dma((10,)), dma((3,)),
        ],
        compiler_params=pltpu.CompilerParams(
            collective_id=0, has_side_effects=True, vmem_limit_bytes=56 * 1024 * 1024
        ),
        cost_estimate=pl.CostEstimate(flops=2_500_000_000, bytes_accessed=4_000_000, transcendentals=262144),
    )(
        neighbour_ids[0].T, neighbour_counts, encoded[0].transpose(1, 2, 0),
        queries.reshape(128, 512), out_grad.reshape(128, 512), key_weight, value_weight,
    )
    grad = jax.ShapeDtypeStruct((4, 4, 56, 256), BF)
    att, qg, kg, vg = pl.pallas_call(
        place,
        out_shape=(low, low, grad, grad),
        in_specs=[vmem] * 4,
        out_specs=(vmem,) * 4,
    )(att, qg, ga, gb)
    return (
        att.reshape(1, 2, 64, 512), qg.reshape(1, 2, 64, 512),
        kg.reshape(896, 256), vg.reshape(896, 256),
    )


def solution(mesh):
    return jax.shard_map(
        body,
        mesh=mesh,
        in_specs=(
            P("dp", "seq", None, "mp"),
            P("dp", "seq", None, "mp"),
            P("dp", None, "seq", "mp"),
            P(None, "mp"),
            P(None, "mp"),
            P("dp", None, None),
            P("dp", "seq"),
        ),
        out_specs=(
            P("dp", "seq", None, "mp"),
            P("dp", "seq", None, "mp"),
            P(None, ("mp", "dp")),
            P(None, ("mp", "dp")),
        ),
        check_vma=False,
    )
```

```python
import functools

import jax
import jax.numpy as jnp
from jax import lax
from jax.experimental import pallas as pl
from jax.experimental.pallas import tpu as pltpu
from jax.sharding import PartitionSpec as P

HD = 128
NX, NZ, NM = 4, 16, 4
MESH = pl.DeviceIdType.MESH
BF = jnp.bfloat16
F32 = jnp.float32
SHIFT = (0, 8, 7, 9, 6, 10, 5, 11, 4, 12, 3, 13, 2, 14, 1, 15)
OTHERS = (2, 1, 3)


def dot(a, b, dims):
    return lax.dot_general(a, b, ((dims[:1], dims[1:]), ((), ())), preferred_element_type=F32)


def wait_bytes(ref, sem):
    pltpu.make_async_copy(ref, ref, sem).wait()


FROM_X = (0, 1, 3, 2)
RA, RB = 32, 24


def kernel(
    ids_ref, counts_ref, enc_ref, q_hbm, og_hbm, wk_hbm, wv_hbm,
    att_hbm, qg_hbm, ga, gb,
    w, q, og, att, qg, outgoing, held, rows, rows_t, kv, sg, dps, dpr,
    ha, hb, xsa, zsb, xra, znb, zfa, zsa, zna, hbx, xsb, xrb, ffa, fsa, fra, ffb, fsb, frb,
    load_sem, send_sem, ax_sem, az_sem, ay_sem, dp_sem, rxa_sem, one_sem, gna_sem,
):
    seq = lax.axis_index("seq")
    m = lax.axis_index("mp")
    d = lax.axis_index("dp")
    x, z = seq // NZ, lax.rem(seq, NZ)
    ze, zj = lax.rem(z, 4), z // 4

    def along_z(k):
        return {"seq": x * NZ + lax.rem(z + k + NZ, NZ)}

    def along_x(k):
        return {"seq": lax.rem(x + k, NX) * NZ + z}

    def along_m(k):
        return {"mp": lax.rem(m + k, NM)}

    sibling = {"dp": 1 - d}

    def send(src, dst, phase, recv, device):
        pltpu.make_async_remote_copy(
            src_ref=src, dst_ref=dst, send_sem=send_sem.at[phase], recv_sem=recv,
            device_id=device, device_id_type=MESH,
        ).start()

    barrier = pltpu.get_barrier_semaphore()
    peers = [along_z(k) for k in range(1, NZ)] + [along_x(k) for k in range(1, NX)]
    peers += [along_m(k) for k in range(1, NM)] + [sibling]
    for peer in peers:
        pl.semaphore_signal(barrier, inc=1, device_id=peer, device_id_type=MESH)

    loads = []
    for e in range(NM):
        for half, hbm in enumerate((wk_hbm, wv_hbm)):
            loads.append(pltpu.make_async_copy(
                hbm.at[pl.ds(224 * e, 224)],
                w.at[pl.ds(256 * e, 224), pl.ds(512 * half, 512)],
                load_sem.at[len(loads)],
            ))
    loads.append(pltpu.make_async_copy(q_hbm, q, load_sem.at[8]))
    loads.append(pltpu.make_async_copy(og_hbm, og, load_sem.at[9]))
    for load in loads:
        load.start()

    lane = lax.broadcasted_iota(jnp.int32, (128, 512), 1)
    part = lax.broadcasted_iota(jnp.int32, (128, 512), 0)
    stretch = (lane // 8) * 2 + (lane // 2) % 2
    wanted = jnp.zeros((8, 512), F32)
    for slot in range(2):
        pick = jnp.where((part == stretch) & (lane % 2 == slot), 1.0, 0.0).astype(BF)
        ids = jnp.broadcast_to(ids_ref[pl.ds(slot, 1), :], (8, 128)).astype(F32).astype(BF)
        wanted += dot(ids, pick, (1, 0))
    wanted = wanted[:1].astype(jnp.int32)
    place = lax.broadcasted_iota(jnp.int32, (256, 512), 0)
    token = (lax.broadcasted_iota(jnp.int32, (1, 512), 1) // 4) % 2
    found = jnp.zeros((224, 512), F32)
    for t in range(2):
        chosen = jnp.where(place == jnp.where(token == t, wanted, -1), 1.0, 0.0).astype(BF)
        found += dot(enc_ref[t], chosen, (1, 0))
    found = jnp.concatenate([found, jnp.zeros((32, 512), F32)], axis=0)
    outgoing[...] = found.T.astype(BF).reshape(NX, NZ, 8, 256)
    held[0] = outgoing[x]

    pl.semaphore_wait(barrier, len(peers))

    for i in (3, 1, 2):
        send(outgoing.at[lax.rem(x + FROM_X[i], NX)], held.at[i], 0, ax_sem.at[i], along_x(FROM_X[i]))
    mine = pl.ds(pl.multiple_of(m * 256, 256), 256)

    def to_z(i):
        if i > 0:
            wait_bytes(held.at[i], ax_sem.at[i])
        for p in range(1, NZ):
            send(held.at[i, lax.rem(z + SHIFT[p], NZ)], rows.at[i, p, :, mine], 1, az_sem.at[i], along_z(SHIFT[p]))
        rows[i, 0, :, mine] = held[i, z]

    def to_m(i):
        wait_bytes(rows.at[i, pl.ds(1, NZ - 1), :, mine], az_sem.at[i])
        for t in OTHERS:
            send(rows.at[i, :, :, mine], rows.at[i, :, :, mine], 2, ay_sem.at[i], along_m(t))

    def project(low, high):
        for i in range(low, high):
            wait_bytes(rows.at[i, :, :, pl.ds(0, 768)], ay_sem.at[i])
        some = pl.ds(128 * low, 128 * (high - low))
        flat = rows[pl.ds(low, high - low)].reshape(128 * (high - low), 1024)
        for c in range(4):
            cols = pl.ds(256 * c, 256)
            kv[some, cols] = dot(flat, w[:, cols], (1, 0)).astype(BF)
        rows_t[:, some] = flat.T

    to_z(0)
    to_z(1)
    to_z(2)
    for e in range(NM):
        w[pl.ds(256 * e + 224, 32), :] = jnp.zeros((32, 1024), BF)
    to_m(0)
    to_z(3)
    for load in loads:
        load.wait()
    for i in range(1, NX):
        to_m(i)
    project(0, 3)
    project(3, 4)

    scale = HD ** (-0.5)
    key = lax.broadcasted_iota(jnp.int32, (128, 512), 1)
    owner = lax.broadcasted_iota(jnp.int32, (128, 512), 0) // 64
    count = jnp.where(owner == 0, counts_ref[0, 0], counts_ref[0, 1])
    valid = (((key // 2) & 1) == owner) & ((key & 1) < count)
    heads = range(4)
    cols = [pl.ds(HD * h, HD) for h in heads]
    vcols = [pl.ds(512 + HD * h, HD) for h in heads]
    qs, gs = [q[:, c] for c in cols], [og[:, c] for c in cols]
    ks, vs = [kv[:, c] for c in cols], [kv[:, c] for c in vcols]
    scores = [jnp.where(valid, dot(qs[h], ks[h], (1, 1)) * scale, -1e30) for h in heads]
    grads = [dot(gs[h], vs[h], (1, 1)) for h in heads]
    expos = [jnp.exp(s - jnp.max(s, axis=-1, keepdims=True)) for s in scores]
    probs = [e * (1.0 / jnp.sum(e, axis=-1, keepdims=True)) for e in expos]
    lows = [p.astype(BF) for p in probs]
    outs = [dot(lows[h], vs[h], (1, 0)) for h in heads]
    value_grads = [dot(lows[h], gs[h], (0, 0)) for h in heads]
    deltas = [jnp.sum(gs[h].astype(F32) * outs[h], axis=-1, keepdims=True) for h in heads]
    grads = [(probs[h] * (grads[h] - deltas[h])).astype(BF) for h in heads]
    key_grads = [dot(grads[h], qs[h], (0, 0)) for h in heads]
    query_grads = [dot(grads[h], ks[h], (1, 0)) for h in heads]
    for h in heads:
        sg[:, cols[h]] = (key_grads[h] * scale).astype(BF)
        sg[:, vcols[h]] = value_grads[h].astype(BF)
    for h in heads:
        att[:, cols[h]] = outs[h].astype(BF)
        qg[:, cols[h]] = (query_grads[h] * scale).astype(BF)
    stores = [
        pltpu.make_async_copy(att, att_hbm, load_sem.at[0]),
        pltpu.make_async_copy(qg, qg_hbm, load_sem.at[1]),
    ]
    for store in stores:
        store.start()

    def partial(e, side, half):
        cols = pl.ds(pl.multiple_of(512 * half + 256 * side, 256), 256)
        return dot(rows_t[pl.ds(256 * e, 256), :], sg[:, cols], (1, 0))[:224]

    def to_class(k, whole, first, second, src, dst, phase, sem):
        @pl.when(k == 1)
        def _():
            send(src(whole), dst(0, whole), phase, sem, along_z(1))

        @pl.when(k == 3)
        def _():
            send(src(whole), dst(1, whole), phase, sem, along_z(-1))

        @pl.when(k == 2)
        def _():
            send(src(first), dst(2, first), phase, sem, along_z(2))
            send(src(second), dst(2, second), phase, sem, along_z(-2))

    whole, first, second = pl.ds(0, 4), pl.ds(0, 2), pl.ds(2, 2)
    for e in range(4):
        for half in range(2):
            part = partial(e, 1 - d, half)
            for c in range(2):
                dps[e, 2 * half + c] = part[:, 128 * c:128 * c + 128].reshape(4, 56, 128).astype(BF)
        send(dps.at[e], dpr.at[e], 3, dp_sem.at[e], sibling)
    for e in range(4):
        parts = [partial(e, d, half) for half in range(2)]
        wait_bytes(dpr.at[e], dp_sem.at[e])
        for half in range(2):
            for c in range(2):
                tile = 2 * half + c
                both = parts[half][:, 128 * c:128 * c + 128].reshape(4, 56, 128) + dpr[e, tile].astype(F32)
                ha[tile, e], hb[e, tile] = both[:, :RA], both[:, RA:]
                xsa[tile, e], zsb[e, tile] = both[:, :RA].astype(BF), both[:, RA:].astype(BF)
        for s in OTHERS:
            send(xsa.at[lax.rem(x + s, NX), e], xra.at[s - 1, e], 4, rxa_sem.at[e], along_x(s))
        to_class(
            lax.rem(e - ze + 4, 4), whole, first, second,
            lambda some: zsb.at[e, some], lambda slot, some: znb.at[slot, some], 5, one_sem.at[0],
        )

    def add(base, received, *where):
        for s in range(3):
            base += received[(s, *where)].astype(F32)
        return base

    def fold_a(e):
        wait_bytes(xra.at[:, e], rxa_sem.at[e])
        total = add(ha[x, e], xra, e)
        zfa[e] = total
        zsa[e] = total.astype(BF)
        to_class(
            lax.rem(e - ze + 4, 4), whole, first, second,
            lambda some: zsa.at[e, some], lambda slot, some: zna.at[slot, some], 6, one_sem.at[1],
        )

    fold_a(0)
    fold_a(1)
    wait_bytes(znb, one_sem.at[0])
    for tile in range(4):
        total = add(hb[ze, tile], znb, tile)
        hbx[tile] = total
        xsb[tile] = total.astype(BF)
    for s in OTHERS:
        send(xsb.at[lax.rem(x + s, NX)], xrb.at[s - 1], 7, one_sem.at[2], along_x(s))
    fold_a(2)
    fold_a(3)
    wait_bytes(xrb, one_sem.at[2])
    total = add(hbx[x], xrb)
    ffb[...] = total
    fsb[...] = total.astype(BF)
    for i in OTHERS:
        send(fsb.at[lax.rem(zj + i, 4)], frb.at[i - 1], 9, one_sem.at[4], along_z(4 * i))
    wait_bytes(zna, one_sem.at[1])
    total = add(zfa[ze], zna)
    ffa[...] = total
    fsa[...] = total.astype(BF)
    for i in OTHERS:
        send(fsa.at[lax.rem(zj + i, 4)], fra.at[i - 1], 8, one_sem.at[3], along_z(4 * i))
    wait_bytes(frb, one_sem.at[4])
    gb[ze, x, zj] = add(ffb[zj], frb).astype(BF)
    for i in OTHERS:
        send(gb.at[ze, x, zj], gb.at[ze, x, zj], 11, one_sem.at[6], along_z(4 * i))
    wait_bytes(fra, one_sem.at[3])
    ga[x, ze, zj] = add(ffa[zj], fra).astype(BF)
    for i in OTHERS:
        send(ga.at[x, ze, zj], ga.at[x, ze, zj], 10, one_sem.at[5], along_z(4 * i))

    wait_bytes(frb, one_sem.at[6])
    for s in OTHERS:
        send(gb.at[ze, x], gb.at[ze, x], 14, one_sem.at[8], along_x(s))
    wait_bytes(fra, one_sem.at[5])
    for i, (shift, some) in enumerate(((2, first), (-2, second), (1, whole), (-1, whole))):
        send(ga.at[x, ze, some], ga.at[x, ze, some], 12, gna_sem.at[max(i - 1, 0)], along_z(shift))
    for s in OTHERS:
        send(ga.at[x, ze], ga.at[x, ze], 13, one_sem.at[7], along_x(s))
    wait_bytes(xrb, one_sem.at[8])
    for shift, some in ((2, first), (-2, second), (1, whole), (-1, whole)):
        send(gb.at[ze, some], gb.at[ze, some], 15, one_sem.at[9], along_z(shift))
    for i, k in ((1, 3), (2, 1), (0, 2)):
        wait_bytes(zna.at[i], gna_sem.at[i])
        group = lax.rem(ze + k, 4)
        for s in OTHERS:
            send(ga.at[x, group], ga.at[x, group], 13, one_sem.at[7], along_x(s))
    wait_bytes(znb, one_sem.at[9])
    wait_bytes(xra, one_sem.at[7])

    for store in stores:
        store.wait()
    wait_bytes(held.at[pl.ds(1, 3)], send_sem.at[0])
    wait_bytes(rows.at[:, pl.ds(1, NZ - 1), :, pl.ds(0, 256)], send_sem.at[1])
    wait_bytes(rows.at[:, :, :, pl.ds(0, 768)], send_sem.at[2])
    for phase, sized in enumerate((dps, xra, znb, zna, xrb, fra, frb, fra, frb, zna, xra, xrb, znb)):
        wait_bytes(sized, send_sem.at[phase + 3])


def place(
    att_in, qg_in, ga, gb, att_out, qg_out, kg_out, vg_out,
    att, qg, ga_in, gb_in, kg, vg, in_sem, out_sem,
):
    pairs = [(att_in, att), (qg_in, qg)]
    for half in range(2):
        for tile in (2 * half, 2 * half + 1):
            pairs += [(ga.at[tile], ga_in.at[tile]), (gb.at[:, tile], gb_in.at[tile])]
    reads = [pltpu.make_async_copy(src, dst, in_sem.at[i]) for i, (src, dst) in enumerate(pairs)]
    pairs = [(kg, kg_out), (vg, vg_out), (att, att_out), (qg, qg_out)]
    writes = [pltpu.make_async_copy(src, dst, out_sem.at[i]) for i, (src, dst) in enumerate(pairs)]
    for read in reads[2:] + reads[:2]:
        read.start()
    for half, out in enumerate((kg, vg)):
        for read in reads[2 + 4 * half:6 + 4 * half]:
            read.wait()
        for c in range(2):
            lanes = pl.ds(128 * c, 128)
            out[:, :, pl.ds(0, RA), lanes] = ga_in[2 * half + c]
            out[:, :, pl.ds(RA, RB), lanes] = gb_in[2 * half + c]
        writes[half].start()
    for i in range(2):
        reads[i].wait()
        writes[2 + i].start()
    for write in writes:
        write.wait()


def body(queries, out_grad, encoded, key_weight, value_weight, neighbour_ids, neighbour_counts):
    vmem = pl.BlockSpec(memory_space=pltpu.VMEM)
    hbm = pl.BlockSpec(memory_space=pl.ANY)
    dma = pltpu.SemaphoreType.DMA

    def bf(*shape):
        return pltpu.VMEM(shape, BF)

    def f32(*shape):
        return pltpu.VMEM(shape, F32)

    low = jax.ShapeDtypeStruct((128, 512), BF)
    att, qg, ga, gb = pl.pallas_call(
        kernel,
        out_shape=(
            low, low,
            jax.ShapeDtypeStruct((4, 4, 4, RA, 128), BF),
            jax.ShapeDtypeStruct((4, 4, 4, RB, 128), BF),
        ),
        in_specs=[vmem, pl.BlockSpec(memory_space=pltpu.SMEM), vmem, hbm, hbm, hbm, hbm],
        out_specs=(hbm, hbm, vmem, vmem),
        scratch_shapes=[
            bf(1024, 1024), bf(128, 512), bf(128, 512), bf(128, 512), bf(128, 512),
            bf(NX, NZ, 8, 256), bf(NX, NZ, 8, 256),
            bf(NX, NZ, 8, 1024), bf(1024, 512), bf(512, 1024), bf(512, 1024),
            bf(4, 4, 4, 56, 128), bf(4, 4, 4, 56, 128),
            f32(4, 4, 4, RA, 128), f32(4, 4, 4, RB, 128),
            bf(4, 4, 4, RA, 128), bf(4, 4, 4, RB, 128),
            bf(3, 4, 4, RA, 128), bf(3, 4, 4, RB, 128),
            f32(4, 4, RA, 128), bf(4, 4, RA, 128), bf(3, 4, RA, 128),
            f32(4, 4, RB, 128), bf(4, 4, RB, 128), bf(3, 4, RB, 128),
            f32(4, RA, 128), bf(4, RA, 128), bf(3, RA, 128),
            f32(4, RB, 128), bf(4, RB, 128), bf(3, RB, 128),
            dma((10,)), dma((16,)), dma((4,)), dma((4,)), dma((4,)),
            dma((4,)), dma((4,)), dma((10,)), dma((3,)),
        ],
        compiler_params=pltpu.CompilerParams(
            collective_id=0, has_side_effects=True, vmem_limit_bytes=56 * 1024 * 1024
        ),
        cost_estimate=pl.CostEstimate(flops=2_500_000_000, bytes_accessed=4_000_000, transcendentals=262144),
    )(
        neighbour_ids[0].T, neighbour_counts, encoded[0].transpose(1, 2, 0),
        queries.reshape(128, 512), out_grad.reshape(128, 512), key_weight, value_weight,
    )
    grad = jax.ShapeDtypeStruct((4, 4, 56, 256), BF)
    att, qg, kg, vg = pl.pallas_call(
        place,
        out_shape=(low, low, grad, grad),
        in_specs=[hbm] * 4,
        out_specs=(hbm,) * 4,
        scratch_shapes=[
            bf(128, 512), bf(128, 512), bf(4, 4, 4, RA, 128), bf(4, 4, 4, RB, 128),
            bf(4, 4, 56, 256), bf(4, 4, 56, 256), dma((10,)), dma((4,)),
        ],
        compiler_params=pltpu.CompilerParams(vmem_limit_bytes=56 * 1024 * 1024),
    )(att, qg, ga, gb)
    return (
        att.reshape(1, 2, 64, 512), qg.reshape(1, 2, 64, 512),
        kg.reshape(896, 256), vg.reshape(896, 256),
    )


def solution(mesh):
    return jax.shard_map(
        body,
        mesh=mesh,
        in_specs=(
            P("dp", "seq", None, "mp"),
            P("dp", "seq", None, "mp"),
            P("dp", None, "seq", "mp"),
            P(None, "mp"),
            P(None, "mp"),
            P("dp", None, None),
            P("dp", "seq"),
        ),
        out_specs=(
            P("dp", "seq", None, "mp"),
            P("dp", "seq", None, "mp"),
            P(None, ("mp", "dp")),
            P(None, ("mp", "dp")),
        ),
        check_vma=False,
    )
```

```python
import functools

import jax
import jax.numpy as jnp
from jax import lax
from jax.experimental import pallas as pl
from jax.experimental.pallas import tpu as pltpu
from jax.sharding import PartitionSpec as P

HD = 128
NX, NZ, NM = 4, 16, 4
MESH = pl.DeviceIdType.MESH
BF = jnp.bfloat16
F32 = jnp.float32
SHIFT = (0, 8, 7, 9, 6, 10, 5, 11, 4, 12, 3, 13, 2, 14, 1, 15)
OTHERS = (2, 1, 3)
RUNS = ((0, 6), (6, 11), (11, 16))


def dot(a, b, dims):
    return lax.dot_general(a, b, ((dims[:1], dims[1:]), ((), ())), preferred_element_type=F32)


def wait_bytes(ref, sem):
    pltpu.make_async_copy(ref, ref, sem).wait()


FROM_X = (0, 1, 3, 2)
RA, RB = 32, 24


def kernel(
    ids_ref, counts_ref, enc_ref, q_hbm, og_hbm, wk_hbm, wv_hbm,
    att_hbm, qg_hbm, ga, gb,
    w, q, og, att, qg, outgoing, held, rows, rows_t, kv, sg, dps, dpr,
    ha, hb, xsa, zsb, xra, znb, zfa, zsa, zna, hbx, xsb, xrb, ffa, fsa, fra, gar, ffb, fsb, frb,
    load_sem, send_sem, ax_sem, az_sem, ay_sem, dp_sem, rxa_sem, one_sem, gza_sem,
):
    seq = lax.axis_index("seq")
    m = lax.axis_index("mp")
    d = lax.axis_index("dp")
    x, z = seq // NZ, lax.rem(seq, NZ)
    ze, zj = lax.rem(z, 4), z // 4

    def along_z(k):
        return {"seq": x * NZ + lax.rem(z + k + NZ, NZ)}

    def along_x(k):
        return {"seq": lax.rem(x + k, NX) * NZ + z}

    def along_m(k):
        return {"mp": lax.rem(m + k, NM)}

    sibling = {"dp": 1 - d}

    def send(src, dst, phase, recv, device):
        pltpu.make_async_remote_copy(
            src_ref=src, dst_ref=dst, send_sem=send_sem.at[phase], recv_sem=recv,
            device_id=device, device_id_type=MESH,
        ).start()

    barrier = pltpu.get_barrier_semaphore()
    peers = [along_z(k) for k in range(1, NZ)] + [along_x(k) for k in range(1, NX)]
    peers += [along_m(k) for k in range(1, NM)] + [sibling]
    for peer in peers:
        pl.semaphore_signal(barrier, inc=1, device_id=peer, device_id_type=MESH)

    loads = []
    for e in range(NM):
        for half, hbm in enumerate((wk_hbm, wv_hbm)):
            loads.append(pltpu.make_async_copy(
                hbm.at[pl.ds(224 * e, 224)],
                w.at[pl.ds(256 * e, 224), pl.ds(512 * half, 512)],
                load_sem.at[len(loads)],
            ))
    loads.append(pltpu.make_async_copy(q_hbm, q, load_sem.at[8]))
    loads.append(pltpu.make_async_copy(og_hbm, og, load_sem.at[9]))
    for load in loads:
        load.start()

    lane = lax.broadcasted_iota(jnp.int32, (128, 512), 1)
    part = lax.broadcasted_iota(jnp.int32, (128, 512), 0)
    stretch = (lane // 8) * 2 + (lane // 2) % 2
    wanted = jnp.zeros((8, 512), F32)
    for slot in range(2):
        pick = jnp.where((part == stretch) & (lane % 2 == slot), 1.0, 0.0).astype(BF)
        ids = jnp.broadcast_to(ids_ref[pl.ds(slot, 1), :], (8, 128)).astype(F32).astype(BF)
        wanted += dot(ids, pick, (1, 0))
    wanted = wanted[:1].astype(jnp.int32)
    place = lax.broadcasted_iota(jnp.int32, (256, 512), 0)
    token = (lax.broadcasted_iota(jnp.int32, (1, 512), 1) // 4) % 2
    found = jnp.zeros((224, 512), F32)
    for t in range(2):
        chosen = jnp.where(place == jnp.where(token == t, wanted, -1), 1.0, 0.0).astype(BF)
        found += dot(enc_ref[t], chosen, (1, 0))
    found = jnp.concatenate([found, jnp.zeros((32, 512), F32)], axis=0)
    outgoing[...] = found.T.astype(BF).reshape(NX, NZ, 8, 256)
    held[0] = outgoing[x]

    pl.semaphore_wait(barrier, len(peers))

    for i in (3, 1, 2):
        send(outgoing.at[lax.rem(x + FROM_X[i], NX)], held.at[i], 0, ax_sem.at[i], along_x(FROM_X[i]))
    mine = pl.ds(pl.multiple_of(m * 256, 256), 256)

    def to_z(i):
        if i > 0:
            wait_bytes(held.at[i], ax_sem.at[i])
        for p in range(1, NZ):
            send(held.at[i, lax.rem(z + SHIFT[p], NZ)], rows.at[i, p, :, mine], 1, az_sem.at[i], along_z(SHIFT[p]))
        rows[i, 0, :, mine] = held[i, z]

    def to_m(i):
        wait_bytes(rows.at[i, pl.ds(1, NZ - 1), :, mine], az_sem.at[i])
        for t in OTHERS:
            send(rows.at[i, :, :, mine], rows.at[i, :, :, mine], 2, ay_sem.at[i], along_m(t))

    def project(low, high):
        for i in range(low, high):
            wait_bytes(rows.at[i, :, :, pl.ds(0, 768)], ay_sem.at[i])
        some = pl.ds(128 * low, 128 * (high - low))
        flat = rows[pl.ds(low, high - low)].reshape(128 * (high - low), 1024)
        for c in range(4):
            cols = pl.ds(256 * c, 256)
            kv[some, cols] = dot(flat, w[:, cols], (1, 0)).astype(BF)
        rows_t[:, some] = flat.T

    to_z(0)
    to_z(1)
    to_z(2)
    for e in range(NM):
        w[pl.ds(256 * e + 224, 32), :] = jnp.zeros((32, 1024), BF)
    to_m(0)
    to_z(3)
    for load in loads:
        load.wait()
    for i in range(1, NX):
        to_m(i)
    project(0, 3)
    project(3, 4)

    scale = HD ** (-0.5)
    key = lax.broadcasted_iota(jnp.int32, (128, 512), 1)
    owner = lax.broadcasted_iota(jnp.int32, (128, 512), 0) // 64
    count = jnp.where(owner == 0, counts_ref[0, 0], counts_ref[0, 1])
    valid = (((key // 2) & 1) == owner) & ((key & 1) < count)
    heads = range(4)
    cols = [pl.ds(HD * h, HD) for h in heads]
    vcols = [pl.ds(512 + HD * h, HD) for h in heads]
    qs, gs = [q[:, c] for c in cols], [og[:, c] for c in cols]
    ks, vs = [kv[:, c] for c in cols], [kv[:, c] for c in vcols]
    scores = [jnp.where(valid, dot(qs[h], ks[h], (1, 1)) * scale, -1e30) for h in heads]
    grads = [dot(gs[h], vs[h], (1, 1)) for h in heads]
    expos = [jnp.exp(s - jnp.max(s, axis=-1, keepdims=True)) for s in scores]
    probs = [e * (1.0 / jnp.sum(e, axis=-1, keepdims=True)) for e in expos]
    lows = [p.astype(BF) for p in probs]
    outs = [dot(lows[h], vs[h], (1, 0)) for h in heads]
    value_grads = [dot(lows[h], gs[h], (0, 0)) for h in heads]
    deltas = [jnp.sum(gs[h].astype(F32) * outs[h], axis=-1, keepdims=True) for h in heads]
    grads = [(probs[h] * (grads[h] - deltas[h])).astype(BF) for h in heads]
    key_grads = [dot(grads[h], qs[h], (0, 0)) for h in heads]
    for h in heads:
        sg[:, cols[h]] = (key_grads[h] * scale).astype(BF)
        sg[:, vcols[h]] = value_grads[h].astype(BF)

    def partial(e, side, half):
        cols = pl.ds(pl.multiple_of(512 * half + 256 * side, 256), 256)
        return dot(rows_t[pl.ds(256 * e, 256), :], sg[:, cols], (1, 0))[:224]

    def to_class(k, whole, first, second, src, dst, phase, sem):
        @pl.when(k == 1)
        def _():
            send(src(whole), dst(0, whole), phase, sem, along_z(1))

        @pl.when(k == 3)
        def _():
            send(src(whole), dst(1, whole), phase, sem, along_z(-1))

        @pl.when(k == 2)
        def _():
            send(src(first), dst(2, first), phase, sem, along_z(2))
            send(src(second), dst(2, second), phase, sem, along_z(-2))

    whole, first, second = pl.ds(0, 4), pl.ds(0, 2), pl.ds(2, 2)
    for e in range(4):
        for half in range(2):
            part = partial(e, 1 - d, half)
            for c in range(2):
                dps[e, 2 * half + c] = part[:, 128 * c:128 * c + 128].reshape(4, 56, 128).astype(BF)
        send(dps.at[e], dpr.at[e], 3, dp_sem.at[e], sibling)
    for h in heads:
        att[:, cols[h]] = outs[h].astype(BF)
        qg[:, cols[h]] = (dot(grads[h], ks[h], (1, 0)) * scale).astype(BF)
    stores = [
        pltpu.make_async_copy(att, att_hbm, load_sem.at[0]),
        pltpu.make_async_copy(qg, qg_hbm, load_sem.at[1]),
    ]
    for store in stores:
        store.start()
    for e in range(4):
        parts = [partial(e, d, half) for half in range(2)]
        wait_bytes(dpr.at[e], dp_sem.at[e])
        for half in range(2):
            for c in range(2):
                tile = 2 * half + c
                both = parts[half][:, 128 * c:128 * c + 128].reshape(4, 56, 128) + dpr[e, tile].astype(F32)
                ha[tile, e], hb[e, tile] = both[:, :RA], both[:, RA:]
                xsa[tile, e], zsb[e, tile] = both[:, :RA].astype(BF), both[:, RA:].astype(BF)
        for s in OTHERS:
            send(xsa.at[lax.rem(x + s, NX), e], xra.at[s - 1, e], 4, rxa_sem.at[e], along_x(s))
        to_class(
            lax.rem(e - ze + 4, 4), whole, first, second,
            lambda some: zsb.at[e, some], lambda slot, some: znb.at[slot, some], 5, one_sem.at[0],
        )

    def add(base, received, *where):
        for s in range(3):
            base += received[(s, *where)].astype(F32)
        return base

    def fold_a(e):
        wait_bytes(xra.at[:, e], rxa_sem.at[e])
        total = add(ha[x, e], xra, e)
        zfa[e] = total
        zsa[e] = total.astype(BF)
        to_class(
            lax.rem(e - ze + 4, 4), whole, first, second,
            lambda some: zsa.at[e, some], lambda slot, some: zna.at[slot, some], 6, one_sem.at[1],
        )

    fold_a(0)
    fold_a(1)
    wait_bytes(znb, one_sem.at[0])
    for tile in range(4):
        total = add(hb[ze, tile], znb, tile)
        hbx[tile] = total
        xsb[tile] = total.astype(BF)
    for s in OTHERS:
        send(xsb.at[lax.rem(x + s, NX)], xrb.at[s - 1], 7, one_sem.at[2], along_x(s))
    fold_a(2)
    fold_a(3)
    wait_bytes(xrb, one_sem.at[2])
    total = add(hbx[x], xrb)
    ffb[...] = total
    fsb[...] = total.astype(BF)
    for i in OTHERS:
        send(fsb.at[lax.rem(zj + i, 4)], frb.at[i - 1], 9, one_sem.at[4], along_z(4 * i))
    wait_bytes(zna, one_sem.at[1])
    total = add(zfa[ze], zna)
    ffa[...] = total
    fsa[...] = total.astype(BF)
    for i in OTHERS:
        send(fsa.at[lax.rem(zj + i, 4)], fra.at[i - 1], 8, one_sem.at[3], along_z(4 * i))
    wait_bytes(frb, one_sem.at[4])
    gb[ze, x, zj] = add(ffb[zj], frb).astype(BF)
    for i in OTHERS:
        send(gb.at[ze, x, zj], gb.at[ze, x, zj], 11, one_sem.at[6], along_z(4 * i))
    wait_bytes(fra, one_sem.at[3])
    gar[x, 0] = add(ffa[zj], fra).astype(BF)
    run_of = [run for run, (low, high) in enumerate(RUNS) for _ in range(low, high)]
    for p in range(1, NZ):
        send(gar.at[x, 0], gar.at[x, p], 10, gza_sem.at[run_of[p]], along_z(SHIFT[p]))

    def spread(run):
        low, high = RUNS[run]
        wait_bytes(gar.at[0, pl.ds(max(low, 1), high - max(low, 1))], gza_sem.at[run])
        for s in OTHERS:
            some = gar.at[x, pl.ds(low, high - low)]
            send(some, some, 13, one_sem.at[7], along_x(s))

    wait_bytes(frb, one_sem.at[6])
    for s in OTHERS:
        send(gb.at[ze, x], gb.at[ze, x], 14, one_sem.at[8], along_x(s))

    def tile_to_z(back):
        tile = gb.at[ze, lax.rem(x + NX - back, NX)]
        for shift in (2 if back % 2 == 0 else -2, 1, -1):
            send(tile, tile, 15, one_sem.at[9], along_z(shift))

    tile_to_z(0)
    spread(0)
    wait_bytes(xrb, one_sem.at[8])
    for back in range(1, NX):
        tile_to_z(back)
    spread(1)
    spread(2)
    wait_bytes(gar.at[pl.ds(0, 3)], one_sem.at[7])
    for p in range(NZ):
        origin = lax.rem(z + NZ - SHIFT[p], NZ)
        ga[:, lax.rem(origin, 4), origin // 4] = gar[:, p]
    wait_bytes(znb, one_sem.at[9])

    for store in stores:
        store.wait()
    wait_bytes(held.at[pl.ds(1, 3)], send_sem.at[0])
    wait_bytes(rows.at[:, pl.ds(1, NZ - 1), :, pl.ds(0, 256)], send_sem.at[1])
    wait_bytes(rows.at[:, :, :, pl.ds(0, 768)], send_sem.at[2])
    sent = (
        (3, dps), (4, xra), (5, znb), (6, zna), (7, xrb), (8, fra), (9, frb), (10, gar.at[0, pl.ds(1, 15)]),
        (11, frb), (13, gar.at[pl.ds(0, 3)]), (14, xrb), (15, znb),
    )
    for phase, sized in sent:
        wait_bytes(sized, send_sem.at[phase])


def place(
    att_in, qg_in, ga, gb, att_out, qg_out, kg_out, vg_out,
    att, qg, ga_in, gb_in, kg, vg, in_sem, out_sem,
):
    pairs = [(att_in, att), (qg_in, qg)]
    for half in range(2):
        for tile in (2 * half, 2 * half + 1):
            pairs += [(ga.at[tile], ga_in.at[tile]), (gb.at[:, tile], gb_in.at[tile])]
    reads = [pltpu.make_async_copy(src, dst, in_sem.at[i]) for i, (src, dst) in enumerate(pairs)]
    pairs = [(kg, kg_out), (vg, vg_out), (att, att_out), (qg, qg_out)]
    writes = [pltpu.make_async_copy(src, dst, out_sem.at[i]) for i, (src, dst) in enumerate(pairs)]
    for read in reads[2:] + reads[:2]:
        read.start()
    for half, out in enumerate((kg, vg)):
        for read in reads[2 + 4 * half:6 + 4 * half]:
            read.wait()
        for c in range(2):
            lanes = pl.ds(128 * c, 128)
            out[:, :, pl.ds(0, RA), lanes] = ga_in[2 * half + c]
            out[:, :, pl.ds(RA, RB), lanes] = gb_in[2 * half + c]
        writes[half].start()
    for i in range(2):
        reads[i].wait()
        writes[2 + i].start()
    for write in writes:
        write.wait()


def body(queries, out_grad, encoded, key_weight, value_weight, neighbour_ids, neighbour_counts):
    vmem = pl.BlockSpec(memory_space=pltpu.VMEM)
    hbm = pl.BlockSpec(memory_space=pl.ANY)
    dma = pltpu.SemaphoreType.DMA

    def bf(*shape):
        return pltpu.VMEM(shape, BF)

    def f32(*shape):
        return pltpu.VMEM(shape, F32)

    low = jax.ShapeDtypeStruct((128, 512), BF)
    att, qg, ga, gb = pl.pallas_call(
        kernel,
        out_shape=(
            low, low,
            jax.ShapeDtypeStruct((4, 4, 4, RA, 128), BF),
            jax.ShapeDtypeStruct((4, 4, 4, RB, 128), BF),
        ),
        in_specs=[vmem, pl.BlockSpec(memory_space=pltpu.SMEM), vmem, hbm, hbm, hbm, hbm],
        out_specs=(hbm, hbm, vmem, vmem),
        scratch_shapes=[
            bf(1024, 1024), bf(128, 512), bf(128, 512), bf(128, 512), bf(128, 512),
            bf(NX, NZ, 8, 256), bf(NX, NZ, 8, 256),
            bf(NX, NZ, 8, 1024), bf(1024, 512), bf(512, 1024), bf(512, 1024),
            bf(4, 4, 4, 56, 128), bf(4, 4, 4, 56, 128),
            f32(4, 4, 4, RA, 128), f32(4, 4, 4, RB, 128),
            bf(4, 4, 4, RA, 128), bf(4, 4, 4, RB, 128),
            bf(3, 4, 4, RA, 128), bf(3, 4, 4, RB, 128),
            f32(4, 4, RA, 128), bf(4, 4, RA, 128), bf(3, 4, RA, 128),
            f32(4, 4, RB, 128), bf(4, 4, RB, 128), bf(3, 4, RB, 128),
            f32(4, RA, 128), bf(4, RA, 128), bf(3, RA, 128),
            bf(4, NZ, RA, 128),
            f32(4, RB, 128), bf(4, RB, 128), bf(3, RB, 128),
            dma((10,)), dma((16,)), dma((4,)), dma((4,)), dma((4,)),
            dma((4,)), dma((4,)), dma((10,)), dma((3,)),
        ],
        compiler_params=pltpu.CompilerParams(
            collective_id=0, has_side_effects=True, vmem_limit_bytes=56 * 1024 * 1024
        ),
        cost_estimate=pl.CostEstimate(flops=2_500_000_000, bytes_accessed=4_000_000, transcendentals=262144),
    )(
        neighbour_ids[0].T, neighbour_counts, encoded[0].transpose(1, 2, 0),
        queries.reshape(128, 512), out_grad.reshape(128, 512), key_weight, value_weight,
    )
    grad = jax.ShapeDtypeStruct((4, 4, 56, 256), BF)
    att, qg, kg, vg = pl.pallas_call(
        place,
        out_shape=(low, low, grad, grad),
        in_specs=[hbm] * 4,
        out_specs=(hbm,) * 4,
        scratch_shapes=[
            bf(128, 512), bf(128, 512), bf(4, 4, 4, RA, 128), bf(4, 4, 4, RB, 128),
            bf(4, 4, 56, 256), bf(4, 4, 56, 256), dma((10,)), dma((4,)),
        ],
        compiler_params=pltpu.CompilerParams(vmem_limit_bytes=56 * 1024 * 1024),
    )(att, qg, ga, gb)
    return (
        att.reshape(1, 2, 64, 512), qg.reshape(1, 2, 64, 512),
        kg.reshape(896, 256), vg.reshape(896, 256),
    )


def solution(mesh):
    return jax.shard_map(
        body,
        mesh=mesh,
        in_specs=(
            P("dp", "seq", None, "mp"),
            P("dp", "seq", None, "mp"),
            P("dp", None, "seq", "mp"),
            P(None, "mp"),
            P(None, "mp"),
            P("dp", None, None),
            P("dp", "seq"),
        ),
        out_specs=(
            P("dp", "seq", None, "mp"),
            P("dp", "seq", None, "mp"),
            P(None, ("mp", "dp")),
            P(None, ("mp", "dp")),
        ),
        check_vma=False,
    )
```

```python
import functools

import jax
import jax.numpy as jnp
from jax import lax
from jax.experimental import pallas as pl
from jax.experimental.pallas import tpu as pltpu
from jax.sharding import PartitionSpec as P

HD = 128
NX, NZ, NM = 4, 16, 4
MESH = pl.DeviceIdType.MESH
BF = jnp.bfloat16
F32 = jnp.float32
SHIFT = (0, 8, 7, 9, 6, 10, 5, 11, 4, 12, 3, 13, 2, 14, 1, 15)
OTHERS = (2, 1, 3)
RUNS = ((0, 6), (6, 10), (10, 13), (13, 16))


def dot(a, b, dims):
    return lax.dot_general(a, b, ((dims[:1], dims[1:]), ((), ())), preferred_element_type=F32)


def wait_bytes(ref, sem):
    pltpu.make_async_copy(ref, ref, sem).wait()


FROM_X = (0, 1, 3, 2)
RA, RB = 32, 24


def kernel(
    ids_ref, counts_ref, enc_ref, q_hbm, og_hbm, wk_hbm, wv_hbm,
    att_hbm, qg_hbm, ga, gb,
    w, q, og, att, qg, outgoing, held, rows, rows_t, kv, sg, dps, dpr,
    ha, hb, xsa, zsb, xra, znb, zfa, zsa, zna, hbx, xsb, xrb, ffa, fsa, fra, gar, ffb, fsb, frb,
    load_sem, send_sem, ax_sem, az_sem, ay_sem, dp_sem, rxa_sem, one_sem, gza_sem,
):
    seq = lax.axis_index("seq")
    m = lax.axis_index("mp")
    d = lax.axis_index("dp")
    x, z = seq // NZ, lax.rem(seq, NZ)
    ze, zj = lax.rem(z, 4), z // 4

    def along_z(k):
        return {"seq": x * NZ + lax.rem(z + k + NZ, NZ)}

    def along_x(k):
        return {"seq": lax.rem(x + k, NX) * NZ + z}

    def along_m(k):
        return {"mp": lax.rem(m + k, NM)}

    sibling = {"dp": 1 - d}

    def send(src, dst, phase, recv, device):
        pltpu.make_async_remote_copy(
            src_ref=src, dst_ref=dst, send_sem=send_sem.at[phase], recv_sem=recv,
            device_id=device, device_id_type=MESH,
        ).start()

    barrier = pltpu.get_barrier_semaphore()
    peers = [along_z(k) for k in range(1, NZ)] + [along_x(k) for k in range(1, NX)]
    peers += [along_m(k) for k in range(1, NM)] + [sibling]
    for peer in peers:
        pl.semaphore_signal(barrier, inc=1, device_id=peer, device_id_type=MESH)

    loads = []
    for e in range(NM):
        for half, hbm in enumerate((wk_hbm, wv_hbm)):
            loads.append(pltpu.make_async_copy(
                hbm.at[pl.ds(224 * e, 224)],
                w.at[pl.ds(256 * e, 224), pl.ds(512 * half, 512)],
                load_sem.at[len(loads)],
            ))
    loads.append(pltpu.make_async_copy(q_hbm, q, load_sem.at[8]))
    loads.append(pltpu.make_async_copy(og_hbm, og, load_sem.at[9]))
    for load in loads:
        load.start()

    lane = lax.broadcasted_iota(jnp.int32, (128, 512), 1)
    part = lax.broadcasted_iota(jnp.int32, (128, 512), 0)
    stretch = (lane // 8) * 2 + (lane // 2) % 2
    wanted = jnp.zeros((8, 512), F32)
    for slot in range(2):
        pick = jnp.where((part == stretch) & (lane % 2 == slot), 1.0, 0.0).astype(BF)
        ids = jnp.broadcast_to(ids_ref[pl.ds(slot, 1), :], (8, 128)).astype(F32).astype(BF)
        wanted += dot(ids, pick, (1, 0))
    wanted = wanted[:1].astype(jnp.int32)
    place = lax.broadcasted_iota(jnp.int32, (256, 512), 0)
    token = (lax.broadcasted_iota(jnp.int32, (1, 512), 1) // 4) % 2
    found = jnp.zeros((224, 512), F32)
    for t in range(2):
        chosen = jnp.where(place == jnp.where(token == t, wanted, -1), 1.0, 0.0).astype(BF)
        found += dot(enc_ref[t], chosen, (1, 0))
    found = jnp.concatenate([found, jnp.zeros((32, 512), F32)], axis=0)
    outgoing[...] = found.T.astype(BF).reshape(NX, NZ, 8, 256)
    held[0] = outgoing[x]

    pl.semaphore_wait(barrier, len(peers))

    for i in (3, 1, 2):
        send(outgoing.at[lax.rem(x + FROM_X[i], NX)], held.at[i], 0, ax_sem.at[i], along_x(FROM_X[i]))
    mine = pl.ds(pl.multiple_of(m * 256, 256), 256)

    def to_z(i):
        if i > 0:
            wait_bytes(held.at[i], ax_sem.at[i])
        for p in range(1, NZ):
            send(held.at[i, lax.rem(z + SHIFT[p], NZ)], rows.at[i, p, :, mine], 1, az_sem.at[i], along_z(SHIFT[p]))
        rows[i, 0, :, mine] = held[i, z]

    def to_m(i):
        wait_bytes(rows.at[i, pl.ds(1, NZ - 1), :, mine], az_sem.at[i])
        for t in OTHERS:
            send(rows.at[i, :, :, mine], rows.at[i, :, :, mine], 2, ay_sem.at[i], along_m(t))

    def project(low, high):
        for i in range(low, high):
            wait_bytes(rows.at[i, :, :, pl.ds(0, 768)], ay_sem.at[i])
        some = pl.ds(128 * low, 128 * (high - low))
        flat = rows[pl.ds(low, high - low)].reshape(128 * (high - low), 1024)
        for c in range(4):
            cols = pl.ds(256 * c, 256)
            kv[some, cols] = dot(flat, w[:, cols], (1, 0)).astype(BF)
        rows_t[:, some] = flat.T

    to_z(0)
    to_z(1)
    to_z(2)
    for e in range(NM):
        w[pl.ds(256 * e + 224, 32), :] = jnp.zeros((32, 1024), BF)
    to_m(0)
    to_z(3)
    for load in loads:
        load.wait()
    for i in range(1, NX):
        to_m(i)
    project(0, 3)
    project(3, 4)

    scale = HD ** (-0.5)
    key = lax.broadcasted_iota(jnp.int32, (128, 512), 1)
    owner = lax.broadcasted_iota(jnp.int32, (128, 512), 0) // 64
    count = jnp.where(owner == 0, counts_ref[0, 0], counts_ref[0, 1])
    valid = (((key // 2) & 1) == owner) & ((key & 1) < count)
    heads = range(4)
    cols = [pl.ds(HD * h, HD) for h in heads]
    vcols = [pl.ds(512 + HD * h, HD) for h in heads]
    qs, gs = [q[:, c] for c in cols], [og[:, c] for c in cols]
    ks, vs = [kv[:, c] for c in cols], [kv[:, c] for c in vcols]
    scores = [jnp.where(valid, dot(qs[h], ks[h], (1, 1)) * scale, -1e30) for h in heads]
    grads = [dot(gs[h], vs[h], (1, 1)) for h in heads]
    expos = [jnp.exp(s - jnp.max(s, axis=-1, keepdims=True)) for s in scores]
    probs = [e * (1.0 / jnp.sum(e, axis=-1, keepdims=True)) for e in expos]
    lows = [p.astype(BF) for p in probs]
    outs = [dot(lows[h], vs[h], (1, 0)) for h in heads]
    value_grads = [dot(lows[h], gs[h], (0, 0)) for h in heads]
    deltas = [jnp.sum(gs[h].astype(F32) * outs[h], axis=-1, keepdims=True) for h in heads]
    grads = [(probs[h] * (grads[h] - deltas[h])).astype(BF) for h in heads]
    key_grads = [dot(grads[h], qs[h], (0, 0)) for h in heads]
    for h in heads:
        sg[:, cols[h]] = (key_grads[h] * scale).astype(BF)
        sg[:, vcols[h]] = value_grads[h].astype(BF)

    def partial(e, side, half):
        cols = pl.ds(pl.multiple_of(512 * half + 256 * side, 256), 256)
        return dot(rows_t[pl.ds(256 * e, 256), :], sg[:, cols], (1, 0))[:224]

    def to_class(k, whole, first, second, src, dst, phase, sem):
        @pl.when(k == 1)
        def _():
            send(src(whole), dst(0, whole), phase, sem, along_z(1))

        @pl.when(k == 3)
        def _():
            send(src(whole), dst(1, whole), phase, sem, along_z(-1))

        @pl.when(k == 2)
        def _():
            send(src(first), dst(2, first), phase, sem, along_z(2))
            send(src(second), dst(2, second), phase, sem, along_z(-2))

    whole, first, second = pl.ds(0, 4), pl.ds(0, 2), pl.ds(2, 2)
    for e in range(4):
        for half in range(2):
            part = partial(e, 1 - d, half)
            for c in range(2):
                dps[e, 2 * half + c] = part[:, 128 * c:128 * c + 128].reshape(4, 56, 128).astype(BF)
        send(dps.at[e], dpr.at[e], 3, dp_sem.at[e], sibling)
    for h in heads:
        att[:, cols[h]] = outs[h].astype(BF)
        qg[:, cols[h]] = (dot(grads[h], ks[h], (1, 0)) * scale).astype(BF)
    stores = [
        pltpu.make_async_copy(att, att_hbm, load_sem.at[0]),
        pltpu.make_async_copy(qg, qg_hbm, load_sem.at[1]),
    ]
    for store in stores:
        store.start()
    for e in range(4):
        parts = [partial(e, d, half) for half in range(2)]
        wait_bytes(dpr.at[e], dp_sem.at[e])
        for half in range(2):
            for c in range(2):
                tile = 2 * half + c
                both = parts[half][:, 128 * c:128 * c + 128].reshape(4, 56, 128) + dpr[e, tile].astype(F32)
                ha[tile, e], hb[e, tile] = both[:, :RA], both[:, RA:]
                xsa[tile, e], zsb[e, tile] = both[:, :RA].astype(BF), both[:, RA:].astype(BF)
        for s in OTHERS:
            send(xsa.at[lax.rem(x + s, NX), e], xra.at[s - 1, e], 4, rxa_sem.at[e], along_x(s))
        to_class(
            lax.rem(e - ze + 4, 4), whole, first, second,
            lambda some: zsb.at[e, some], lambda slot, some: znb.at[slot, some], 5, one_sem.at[0],
        )

    def add(base, received, *where):
        for s in range(3):
            base += received[(s, *where)].astype(F32)
        return base

    def fold_a(e):
        wait_bytes(xra.at[:, e], rxa_sem.at[e])
        total = add(ha[x, e], xra, e)
        zfa[e] = total
        zsa[e] = total.astype(BF)
        to_class(
            lax.rem(e - ze + 4, 4), whole, first, second,
            lambda some: zsa.at[e, some], lambda slot, some: zna.at[slot, some], 6, one_sem.at[1],
        )

    fold_a(0)
    fold_a(1)
    wait_bytes(znb, one_sem.at[0])
    for tile in range(4):
        total = add(hb[ze, tile], znb, tile)
        hbx[tile] = total
        xsb[tile] = total.astype(BF)
    for s in OTHERS:
        send(xsb.at[lax.rem(x + s, NX)], xrb.at[s - 1], 7, one_sem.at[2], along_x(s))
    fold_a(2)
    fold_a(3)
    wait_bytes(xrb, one_sem.at[2])
    total = add(hbx[x], xrb)
    ffb[...] = total
    fsb[...] = total.astype(BF)
    for i in OTHERS:
        send(fsb.at[lax.rem(zj + i, 4)], frb.at[i - 1], 9, one_sem.at[4], along_z(4 * i))
    wait_bytes(zna, one_sem.at[1])
    total = add(zfa[ze], zna)
    ffa[...] = total
    fsa[...] = total.astype(BF)
    for i in OTHERS:
        send(fsa.at[lax.rem(zj + i, 4)], fra.at[i - 1], 8, one_sem.at[3], along_z(4 * i))
    wait_bytes(frb, one_sem.at[4])
    gb[ze, x, zj] = add(ffb[zj], frb).astype(BF)
    for i in OTHERS:
        send(gb.at[ze, x, zj], gb.at[ze, x, zj], 11, one_sem.at[6], along_z(4 * i))
    wait_bytes(fra, one_sem.at[3])
    gar[x, 0] = add(ffa[zj], fra).astype(BF)
    run_of = [run for run, (low, high) in enumerate(RUNS) for _ in range(low, high)]
    for p in range(1, NZ):
        send(gar.at[x, 0], gar.at[x, p], 10, gza_sem.at[run_of[p]], along_z(SHIFT[p]))

    def spread(run):
        low, high = RUNS[run]
        wait_bytes(gar.at[0, pl.ds(max(low, 1), high - max(low, 1))], gza_sem.at[run])
        for s in OTHERS:
            some = gar.at[x, pl.ds(low, high - low)]
            send(some, some, 13, one_sem.at[7], along_x(s))

    wait_bytes(frb, one_sem.at[6])
    for s in OTHERS:
        send(gb.at[ze, x], gb.at[ze, x], 14, one_sem.at[8], along_x(s))

    def tile_to_z(back):
        tile = gb.at[ze, lax.rem(x + NX - back, NX)]
        for shift in (2 if back % 2 == 0 else -2, 1, -1):
            send(tile, tile, 15, one_sem.at[9], along_z(shift))

    tile_to_z(0)
    spread(0)
    wait_bytes(xrb, one_sem.at[8])
    for back in range(1, NX):
        tile_to_z(back)
    for run in range(1, len(RUNS)):
        spread(run)
    wait_bytes(gar.at[pl.ds(0, 3)], one_sem.at[7])
    for p in range(NZ):
        origin = lax.rem(z + NZ - SHIFT[p], NZ)
        ga[:, lax.rem(origin, 4), origin // 4] = gar[:, p]
    wait_bytes(znb, one_sem.at[9])

    for store in stores:
        store.wait()
    wait_bytes(held.at[pl.ds(1, 3)], send_sem.at[0])
    wait_bytes(rows.at[:, pl.ds(1, NZ - 1), :, pl.ds(0, 256)], send_sem.at[1])
    wait_bytes(rows.at[:, :, :, pl.ds(0, 768)], send_sem.at[2])
    sent = (
        (3, dps), (4, xra), (5, znb), (6, zna), (7, xrb), (8, fra), (9, frb), (10, gar.at[0, pl.ds(1, 15)]),
        (11, frb), (13, gar.at[pl.ds(0, 3)]), (14, xrb), (15, znb),
    )
    for phase, sized in sent:
        wait_bytes(sized, send_sem.at[phase])


def place(
    att_in, qg_in, ga, gb, att_out, qg_out, kg_out, vg_out,
    att, qg, ga_in, gb_in, kg, vg, in_sem, out_sem,
):
    pairs = [(att_in, att), (qg_in, qg)]
    for half in range(2):
        for tile in (2 * half, 2 * half + 1):
            pairs += [(ga.at[tile], ga_in.at[tile]), (gb.at[:, tile], gb_in.at[tile])]
    reads = [pltpu.make_async_copy(src, dst, in_sem.at[i]) for i, (src, dst) in enumerate(pairs)]
    pairs = [(kg, kg_out), (vg, vg_out), (att, att_out), (qg, qg_out)]
    writes = [pltpu.make_async_copy(src, dst, out_sem.at[i]) for i, (src, dst) in enumerate(pairs)]
    for read in reads[2:] + reads[:2]:
        read.start()
    for half, out in enumerate((kg, vg)):
        for read in reads[2 + 4 * half:6 + 4 * half]:
            read.wait()
        for c in range(2):
            lanes = pl.ds(128 * c, 128)
            out[:, :, pl.ds(0, RA), lanes] = ga_in[2 * half + c]
            out[:, :, pl.ds(RA, RB), lanes] = gb_in[2 * half + c]
        writes[half].start()
    for i in range(2):
        reads[i].wait()
        writes[2 + i].start()
    for write in writes:
        write.wait()


def body(queries, out_grad, encoded, key_weight, value_weight, neighbour_ids, neighbour_counts):
    vmem = pl.BlockSpec(memory_space=pltpu.VMEM)
    hbm = pl.BlockSpec(memory_space=pl.ANY)
    dma = pltpu.SemaphoreType.DMA

    def bf(*shape):
        return pltpu.VMEM(shape, BF)

    def f32(*shape):
        return pltpu.VMEM(shape, F32)

    low = jax.ShapeDtypeStruct((128, 512), BF)
    att, qg, ga, gb = pl.pallas_call(
        kernel,
        out_shape=(
            low, low,
            jax.ShapeDtypeStruct((4, 4, 4, RA, 128), BF),
            jax.ShapeDtypeStruct((4, 4, 4, RB, 128), BF),
        ),
        in_specs=[vmem, pl.BlockSpec(memory_space=pltpu.SMEM), vmem, hbm, hbm, hbm, hbm],
        out_specs=(hbm, hbm, vmem, vmem),
        scratch_shapes=[
            bf(1024, 1024), bf(128, 512), bf(128, 512), bf(128, 512), bf(128, 512),
            bf(NX, NZ, 8, 256), bf(NX, NZ, 8, 256),
            bf(NX, NZ, 8, 1024), bf(1024, 512), bf(512, 1024), bf(512, 1024),
            bf(4, 4, 4, 56, 128), bf(4, 4, 4, 56, 128),
            f32(4, 4, 4, RA, 128), f32(4, 4, 4, RB, 128),
            bf(4, 4, 4, RA, 128), bf(4, 4, 4, RB, 128),
            bf(3, 4, 4, RA, 128), bf(3, 4, 4, RB, 128),
            f32(4, 4, RA, 128), bf(4, 4, RA, 128), bf(3, 4, RA, 128),
            f32(4, 4, RB, 128), bf(4, 4, RB, 128), bf(3, 4, RB, 128),
            f32(4, RA, 128), bf(4, RA, 128), bf(3, RA, 128),
            bf(4, NZ, RA, 128),
            f32(4, RB, 128), bf(4, RB, 128), bf(3, RB, 128),
            dma((10,)), dma((16,)), dma((4,)), dma((4,)), dma((4,)),
            dma((4,)), dma((4,)), dma((10,)), dma((len(RUNS),)),
        ],
        compiler_params=pltpu.CompilerParams(
            collective_id=0, has_side_effects=True, vmem_limit_bytes=56 * 1024 * 1024
        ),
        cost_estimate=pl.CostEstimate(flops=2_500_000_000, bytes_accessed=4_000_000, transcendentals=262144),
    )(
        neighbour_ids[0].T, neighbour_counts, encoded[0].transpose(1, 2, 0),
        queries.reshape(128, 512), out_grad.reshape(128, 512), key_weight, value_weight,
    )
    grad = jax.ShapeDtypeStruct((4, 4, 56, 256), BF)
    att, qg, kg, vg = pl.pallas_call(
        place,
        out_shape=(low, low, grad, grad),
        in_specs=[hbm] * 4,
        out_specs=(hbm,) * 4,
        scratch_shapes=[
            bf(128, 512), bf(128, 512), bf(4, 4, 4, RA, 128), bf(4, 4, 4, RB, 128),
            bf(4, 4, 56, 256), bf(4, 4, 56, 256), dma((10,)), dma((4,)),
        ],
        compiler_params=pltpu.CompilerParams(vmem_limit_bytes=56 * 1024 * 1024),
    )(att, qg, ga, gb)
    return (
        att.reshape(1, 2, 64, 512), qg.reshape(1, 2, 64, 512),
        kg.reshape(896, 256), vg.reshape(896, 256),
    )


def solution(mesh):
    return jax.shard_map(
        body,
        mesh=mesh,
        in_specs=(
            P("dp", "seq", None, "mp"),
            P("dp", "seq", None, "mp"),
            P("dp", None, "seq", "mp"),
            P(None, "mp"),
            P(None, "mp"),
            P("dp", None, None),
            P("dp", "seq"),
        ),
        out_specs=(
            P("dp", "seq", None, "mp"),
            P("dp", "seq", None, "mp"),
            P(None, ("mp", "dp")),
            P(None, ("mp", "dp")),
        ),
        check_vma=False,
    )
```
